32 devices in a mesh: group: 2 (over y), dp: 4 (over x, core), mp: 4 (over z).
Axes of the slice: x: 2, y: 2, z: 4, core: 2. Of those that a mesh axis runs over, the one named last changes fastest.
Arguments:
- tokens: bfloat16 [2048, 6144], P(('group', 'dp'), 'mp'), parts along dimension 0, may hold values from -40 to 40, as said below
- counts: int32 [8, 4, 2], P('group'), parts along dimension 0, may hold values from 1 to 48, 64 in all within a row
- ln_gain: float32 [6144], replicated, may hold values from 0.1 to 1.9
- w_qkv: bfloat16 [6144, 3, 3072], P('dp', None, 'mp'), may hold values from -0.078125 to 0.078125
- w_up: bfloat16 [6144, 12288], P('dp', 'mp'), may hold values from -0.078125 to 0.078125
- w_out: bfloat16 [3072, 6144], P('dp', 'mp'), may hold values from -0.109375 to 0.109375
- w_down: bfloat16 [12288, 6144], P('dp', 'mp'), may hold values from -0.0546875 to 0.0546875
Outputs:
- mixed: bfloat16 [2048, 6144], P(('group', 'dp'), 'mp'), parts along dimension 0
The draws below stay inside these ranges and needn't reach their ends.
There are 2 independent parts, one for each index of `group`. The reference program is written for one: setup_inputs(seed, part) draws one part's arguments, and reference() takes and returns one part's arrays. A program takes and returns all parts, laid end to end along the dimension named above; an argument that names none is the same for every part. Nothing has to cross between parts.
Inputs may be any that keep to these rules, and one draw needn't show every extreme that they name: tokens have feature and row scales that differ. `counts`: each region of 64 rows is filled exactly by its 2 images.
All inputs are finite; a program needn't handle non-finite values.
Results may differ from the reference program's by a relative error of at most 0.0031.
Values may be sent and summed in bfloat16 or wider, within the bound.
A program may use at most 256 MiB of HBM per device.

```python
import math
import jax
import jax.numpy as jnp
import numpy as np
from jax import lax

D = 6144
HEADS = 24
HDIM = 128
F = 12288
CAP = 64
IMGS = 2
HD = 3072
MOSTP = 48
TOKENS = 1024
N_DP = 4


def draw_tokens(key, part):
    key = jax.random.fold_in(key, 11)
    key_base, key_col, key_row = jax.random.split(key, 3)
    column = jnp.exp(jax.random.uniform(key_col, (D,), jnp.float32, math.log(0.5), math.log(5.0)))
    row = jnp.exp(jax.random.uniform(key_row, (TOKENS, 1), jnp.float32, math.log(0.5), math.log(2.0)))
    base = jax.random.normal(key_base, (TOKENS, D), jnp.float32)
    base = jnp.clip(base, -4.0, 4.0)
    return (base * column[None, :] * row).astype(jnp.bfloat16)


def levels(own_key, shape, pieces, low, top_value):
    level = 1.0
    for dim, shards_of in pieces:
        steps = jax.random.uniform(jax.random.fold_in(jax.random.fold_in(own_key, 6), dim), (shards_of,), jnp.float32, low / len(pieces), top_value / len(pieces))
        level = level * jnp.repeat(jnp.exp(steps), shape[dim] // shards_of).reshape((-1,) + (1,) * (len(shape) - 1 - dim))
    return level


def length_profile(count, total, bound, skew):
    weights = [(1 << 20) // math.isqrt(standing ** skew) + 1 for standing in range(2, count + 1)]
    surplus, holding = total - bound - (count - 1), [1] * (count - 1)
    while surplus > 0:
        candidates = [i for i in range(count - 1) if holding[i] < bound]
        whole, left = sum([weights[i] for i in candidates]), surplus
        for i in candidates:
            extra = min(bound - holding[i], max(1, left * weights[i] // whole), surplus)
            holding[i] = holding[i] + extra
            surplus = surplus - extra
    return np.array([bound] + holding)


def ragged_sizes(rng, number_of, total, most, skew):
    if number_of == 2:
        one = jax.random.randint(rng, (), max(1, total - most), min(most, total - 1) + 1)
        return jnp.stack([one, total - one])
    lengths = jnp.asarray(length_profile(number_of, total, most, skew), jnp.int32)
    twos = (number_of - 1) // 2
    source_of, taker = lengths[1:1 + 2 * twos:2], lengths[2:2 + 2 * twos:2]
    room = jnp.minimum(source_of - 1, most - taker)
    shifted = jax.random.randint(jax.random.fold_in(rng, 1), (twos,), 0, 1 << 20) % (room + 1)
    lengths = lengths.at[1:1 + 2 * twos:2].set(source_of - shifted).at[2:2 + 2 * twos:2].set(taker + shifted)
    return lengths[jax.random.permutation(jax.random.fold_in(rng, 2), number_of)]


def gaussian(key, extent, width, most, cuts=(), kind=jnp.bfloat16):
    result = width * jax.random.normal(key, extent, jnp.float32)
    if cuts:
        result = result * levels(key, extent, cuts, -0.22, 0.18)
    return jnp.clip(result, -most, most).astype(kind)


def setup_inputs(seed: int = 0, part: int = 0) -> dict:
    key_of = jax.random.split(jax.random.key(seed), 8)
    part_splits = jax.random.split(jax.random.fold_in(key_of[7], part), 8)
    return {
        "tokens": draw_tokens(jax.random.fold_in(jax.random.fold_in(key_of[7], part), 71), part),
        "counts": jax.vmap(lambda own: ragged_sizes(own, IMGS, CAP, MOSTP, 2))(jax.random.split(part_splits[1], N_DP * N_DP)).reshape((N_DP, N_DP, IMGS)).astype(jnp.int32),
        "ln_gain": jnp.clip(1.0 + 0.18 * jax.random.normal(key_of[2], (D,), jnp.float32), 0.1, 1.9),
        "w_qkv": gaussian(key_of[3], (D, 3, HD), D ** -0.5, 0.078125, ((0, 4), (2, 4))),
        "w_up": gaussian(key_of[4], (D, F), D ** -0.5, 0.078125, ((0, 4), (1, 4))),
        "w_out": gaussian(key_of[5], (HD, D), HD ** -0.5, 0.109375, ((0, 4), (1, 4))),
        "w_down": gaussian(key_of[6], (F, D), F ** -0.5, 0.0546875, ((0, 4), (1, 4))),
    }


def layer_norm(values, eps):
    mean = lax.optimization_barrier(jnp.mean(values, axis=-1, keepdims=True))
    centred = values - mean
    variance = lax.optimization_barrier(jnp.mean(centred * centred, axis=-1, keepdims=True))
    return centred * lax.rsqrt(variance + eps)

def image_ids(counts):
    bounds = jnp.cumsum(counts, axis=-1).astype(jnp.int32)
    position = jnp.arange(CAP).astype(jnp.int32)
    segment = lax.optimization_barrier(jnp.sum((position[None, None, :, None] >= bounds[:, :, None, :]).astype(jnp.int32), axis=-1)).astype(jnp.int32)
    sender = jnp.arange(N_DP).astype(jnp.int32)[:, None, None]
    receiver = jnp.arange(N_DP).astype(jnp.int32)[None, :, None]
    ident = ((receiver * N_DP + sender) * IMGS + segment).astype(jnp.int32)
    return jnp.transpose(ident, (1, 0, 2)).reshape(TOKENS)

def reference(tokens, counts, ln_gain, w_qkv, w_up, w_out, w_down):
    moved = jnp.transpose(tokens.reshape(N_DP, N_DP, CAP, D), (1, 0, 2, 3)).reshape(TOKENS, D)
    ident = image_ids(counts)
    wide = moved.astype(jnp.float32)
    normed = (layer_norm(wide, 1e-06) * ln_gain.astype(jnp.float32)).astype(jnp.bfloat16)
    qkv = jnp.dot(normed, w_qkv.reshape(D, 3 * HD), preferred_element_type=jnp.float32).astype(jnp.bfloat16)
    qkv = qkv.reshape(TOKENS, 3, HEADS, HDIM)
    query_n = layer_norm(qkv[:, 0].astype(jnp.float32), 1e-06).astype(jnp.bfloat16)
    key_n = layer_norm(qkv[:, 1].astype(jnp.float32), 1e-06).astype(jnp.bfloat16)
    values = qkv[:, 2]
    scores = jnp.einsum('qhd,khd->hqk', query_n.astype(jnp.float32), key_n.astype(jnp.float32)) * (1.0 / HDIM ** 0.5)
    same = (ident[:, None] == ident[None, :]).astype(jnp.float32)
    probs = jnp.exp(scores) * same[None]
    weights = (probs / lax.optimization_barrier(jnp.sum(probs, axis=-1, keepdims=True))).astype(jnp.bfloat16)
    attended = jnp.einsum('hqk,khd->qhd', weights.astype(jnp.float32), values.astype(jnp.float32)).astype(jnp.bfloat16)
    attended = attended.reshape(TOKENS, HD)
    hidden = jax.nn.gelu(jnp.dot(normed, w_up, preferred_element_type=jnp.float32), approximate=False).astype(jnp.bfloat16)
    mixed = wide + jnp.dot(attended, w_out, preferred_element_type=jnp.float32) + jnp.dot(hidden, w_down, preferred_element_type=jnp.float32)
    return mixed.astype(jnp.bfloat16)
```

```python
import jax
import jax.numpy as jnp
from jax import lax
from jax.sharding import PartitionSpec as P

HDIM = 128
IMGS = 2


def layer_norm(values, eps):
    mean = jnp.mean(values, axis=-1, keepdims=True)
    centred = values - mean
    variance = jnp.mean(centred * centred, axis=-1, keepdims=True)
    return centred * lax.rsqrt(variance + eps)


def attend(qkv, same):
    senders, region, _, width = qkv.shape
    heads = width // HDIM
    query_raw, key_raw, values = (
        qkv[:, :, part].reshape(senders, region, heads, HDIM) for part in range(3)
    )
    query_n = layer_norm(query_raw.astype(jnp.float32), 1e-06).astype(jnp.bfloat16)
    key_n = layer_norm(key_raw.astype(jnp.float32), 1e-06).astype(jnp.bfloat16)
    scores = jnp.einsum(
        "sqhd,skhd->shqk", query_n, key_n, preferred_element_type=jnp.float32
    ) * (1.0 / HDIM**0.5)
    probs = jnp.exp(scores) * same[:, None]
    weights = (probs / jnp.sum(probs, axis=-1, keepdims=True)).astype(jnp.bfloat16)
    result = jnp.einsum(
        "shqk,skhd->sqhd", weights, values, preferred_element_type=jnp.float32
    ).astype(jnp.bfloat16)
    return result.reshape(senders * region, width)


def exchange(values, n_dp, step):
    return lax.ppermute(values, "dp", [(index, index ^ step) for index in range(n_dp)])


def pick(values, index, size):
    return lax.dynamic_slice_in_dim(values, index, size, axis=0)


def sum_scatter(partial, n_dp):
    me = lax.axis_index("dp")
    assert n_dp & (n_dp - 1) == 0
    rest = partial.reshape(partial.shape[0], *partial.shape[1:])
    step = 1
    while step < n_dp:
        bit = (me // step) % 2
        halves = rest.reshape(rest.shape[0] // 2, 2, *rest.shape[1:])
        keep = lax.dynamic_index_in_dim(halves, bit, axis=1, keepdims=False)
        send = lax.dynamic_index_in_dim(halves, 1 - bit, axis=1, keepdims=False)
        got = exchange(send.astype(jnp.bfloat16), n_dp, step)
        rest = keep.astype(jnp.float32) + got.astype(jnp.float32)
        step *= 2
    return rest[0]


def make(n_dp, n_mp):
    def shards(tokens, counts, ln_gain, w_qkv, w_up, w_out, w_down):
        rows, cols = tokens.shape
        depth, _, part_cols = w_qkv.shape
        senders = counts.shape[0]
        region = rows // senders
        me = lax.axis_index("dp")

        whole = lax.all_gather(tokens, "mp", axis=1, tiled=True)
        normed = (layer_norm(whole.astype(jnp.float32), 1e-06) * ln_gain).astype(jnp.bfloat16)
        fed = lax.all_to_all(normed, "dp", split_axis=1, concat_axis=0, tiled=True)
        fed = fed.reshape(senders, n_dp, region, depth).transpose(1, 0, 2, 3)
        fed = fed.reshape(n_dp * rows, depth)
        moved = lax.all_to_all(tokens, "dp", split_axis=0, concat_axis=0, tiled=True)

        qkv_sum = jnp.dot(
            fed, w_qkv.reshape(depth, 3 * part_cols), preferred_element_type=jnp.float32
        )
        qkv = sum_scatter(qkv_sum.reshape(n_dp, rows, 3 * part_cols), n_dp).astype(jnp.bfloat16)
        up_sum = jnp.dot(fed, w_up, preferred_element_type=jnp.float32)
        hidden = jax.nn.gelu(
            sum_scatter(up_sum.reshape(n_dp, rows, up_sum.shape[1]), n_dp), approximate=False
        ).astype(jnp.bfloat16)

        mine = lax.dynamic_index_in_dim(counts, me, axis=1, keepdims=False)
        bounds = jnp.cumsum(mine, axis=-1)
        position = jnp.arange(region)
        segment = jnp.sum((position[None, :, None] >= bounds[:, None, :]).astype(jnp.int32), axis=-1)
        same = (segment[:, :, None] == segment[:, None, :]).astype(jnp.float32)

        qkv = qkv.reshape(rows, 3, part_cols)
        if part_cols % HDIM:
            qkv = lax.all_gather(qkv, "mp", axis=2, tiled=True)
            attended = attend(qkv.reshape(senders, region, 3, qkv.shape[2]), same)
        else:
            attended = attend(qkv.reshape(senders, region, 3, part_cols), same)
            attended = lax.all_gather(attended, "mp", axis=1, tiled=True)
        hidden = lax.all_gather(hidden, "mp", axis=1, tiled=True)
        attended = lax.all_to_all(attended, "dp", split_axis=1, concat_axis=0, tiled=True)
        hidden = lax.all_to_all(hidden, "dp", split_axis=1, concat_axis=0, tiled=True)

        mixed = jnp.dot(attended, w_out, preferred_element_type=jnp.float32)
        mixed = mixed + jnp.dot(hidden, w_down, preferred_element_type=jnp.float32)
        mixed = sum_scatter(mixed.reshape(n_dp, rows, cols), n_dp)
        return (moved.astype(jnp.float32) + mixed).astype(jnp.bfloat16)

    return shards


def solution(mesh):
    return jax.shard_map(
        make(mesh.shape["dp"], mesh.shape["mp"]),
        mesh=mesh,
        in_specs=(
            P(("group", "dp"), "mp"),
            P("group", None, None),
            P(),
            P("dp", None, "mp"),
            P("dp", "mp"),
            P("dp", "mp"),
            P("dp", "mp"),
        ),
        out_specs=P(("group", "dp"), "mp"),
        check_vma=False,
    )
```

```python
import jax
import jax.numpy as jnp
from jax import lax
from jax.sharding import PartitionSpec as P

HDIM = 128
IMGS = 2
CHUNKS = 2


def layer_norm(values, eps, axes):
    mean = jnp.mean(values, axis=axes, keepdims=True)
    centred = values - mean
    variance = jnp.mean(centred * centred, axis=axes, keepdims=True)
    return centred * lax.rsqrt(variance + eps)


def attend(qkv, same):
    senders, region, _, width = qkv.shape
    heads = width // HDIM
    query_raw, key_raw, values = (
        qkv[:, :, part].reshape(senders, region, heads, HDIM) for part in range(3)
    )
    query_n = layer_norm(query_raw.astype(jnp.float32), 1e-06, -1).astype(jnp.bfloat16)
    key_n = layer_norm(key_raw.astype(jnp.float32), 1e-06, -1).astype(jnp.bfloat16)
    scores = jnp.einsum(
        "sqhd,skhd->shqk", query_n, key_n, preferred_element_type=jnp.float32
    ) * (1.0 / HDIM**0.5)
    probs = jnp.exp(scores) * same[:, None]
    weights = (probs / jnp.sum(probs, axis=-1, keepdims=True)).astype(jnp.bfloat16)
    result = jnp.einsum(
        "shqk,skhd->sqhd", weights, values, preferred_element_type=jnp.float32
    ).astype(jnp.bfloat16)
    return result.reshape(senders, region, width)


def exchange(values, n_dp, step):
    return lax.ppermute(values, "dp", [(index, index ^ step) for index in range(n_dp)])


def relative(values, me):
    count = values.shape[0]
    return [lax.dynamic_index_in_dim(values, me ^ j, 0, keepdims=False) for j in range(count)]


def product_sum(blocks, weights, n_dp):
    far = jnp.concatenate([blocks[3], blocks[1]], axis=0)
    near = jnp.concatenate([blocks[2], blocks[0]], axis=0)
    rows = blocks[0].shape[0]
    sent = jnp.dot(far, weights, preferred_element_type=jnp.float32).astype(jnp.bfloat16)
    got = exchange(sent, n_dp, 1)
    kept = jnp.dot(near, weights, preferred_element_type=jnp.float32)
    across = (kept[:rows] + got[:rows].astype(jnp.float32)).astype(jnp.bfloat16)
    across = exchange(across, n_dp, 2)
    return kept[rows:] + got[rows:].astype(jnp.float32) + across.astype(jnp.float32)


def make(n_dp, n_mp):
    assert n_dp == 4 and n_mp % n_dp == 0
    each = n_mp // n_dp

    def gather_spread(values, me):
        rows, cols = values.shape
        gathered = lax.all_gather(values, "mp", axis=0, tiled=False)
        gathered = gathered.reshape(n_dp, each, rows, cols)
        parts = relative(gathered, me)
        got = [parts[0]] + [exchange(parts[k], n_dp, k) for k in range(1, n_dp)]
        return [part.transpose(1, 0, 2).reshape(rows, each * cols) for part in got]

    def shards(tokens, counts, ln_gain, w_qkv, w_up, w_out, w_down):
        rows, cols = tokens.shape
        depth, _, part_cols = w_qkv.shape
        senders = counts.shape[0]
        region = rows // senders
        piece = region // CHUNKS
        me = lax.axis_index("dp")
        w_qkv = w_qkv.reshape(depth, 3 * part_cols)

        by_receiver = relative(tokens.reshape(senders, region, cols), me)
        own = jnp.stack(by_receiver, axis=0)
        gain = ln_gain.reshape(n_dp, each, 1, 1, cols)

        def feed(chunk):
            mine = own[:, chunk * piece : (chunk + 1) * piece].reshape(senders * piece, cols)
            gathered = lax.all_gather(mine, "mp", axis=0, tiled=False)
            gathered = gathered.reshape(n_dp, each, senders * piece, cols)
            normed = layer_norm(gathered.astype(jnp.float32), 1e-06, (0, 1, 3))
            normed = (normed * gain.reshape(n_dp, each, 1, cols)).astype(jnp.bfloat16)
            parts = relative(normed, me)
            got = [parts[0]] + [exchange(parts[k], n_dp, k) for k in range(1, n_dp)]
            got = [
                part.transpose(1, 0, 2).reshape(senders, piece, each * cols) for part in got
            ]
            return [
                jnp.concatenate([got[j ^ i][i] for i in range(senders)], axis=0)
                for j in range(n_dp)
            ]

        fed, hidden, qkv = [], [], []
        for chunk in range(CHUNKS):
            fed.append(feed(chunk))
        moved = [by_receiver[0]] + [exchange(by_receiver[i], n_dp, i) for i in range(1, senders)]
        moved = jnp.stack(moved, axis=0)

        for chunk in range(CHUNKS):
            part = product_sum(fed[chunk], w_up, n_dp)
            hidden.append(jax.nn.gelu(part, approximate=False).astype(jnp.bfloat16))
            part = product_sum(fed[chunk], w_qkv, n_dp).astype(jnp.bfloat16)
            qkv.append(part.reshape(senders, piece, 3, part_cols))

        order = jnp.arange(senders) ^ me
        theirs = lax.dynamic_index_in_dim(counts, me, axis=1, keepdims=False)[order]
        bounds = jnp.cumsum(theirs, axis=-1)
        position = jnp.arange(region)
        segment = jnp.sum((position[None, :, None] >= bounds[:, None, :]).astype(jnp.int32), axis=-1)
        same = (segment[:, :, None] == segment[:, None, :]).astype(jnp.float32)

        qkv = jnp.concatenate(qkv, axis=1)
        if part_cols % HDIM:
            everything = lax.all_gather(qkv, "mp", axis=3, tiled=True)
            attended = attend(everything, same)
            attended = lax.dynamic_slice_in_dim(
                attended, lax.axis_index("mp") * part_cols, part_cols, axis=2
            )
        else:
            attended = attend(qkv, same)

        attended, moved = lax.optimization_barrier((attended, moved))
        spread = [gather_spread(part, me) for part in hidden[:-1]]
        looked = gather_spread(attended.reshape(rows, part_cols), me)
        spread.append(gather_spread(hidden[-1], me))
        out = []
        for chunk in range(CHUNKS):
            blocks = []
            for j in range(n_dp):
                seen = looked[j].reshape(senders, region, -1)
                seen = seen[:, chunk * piece : (chunk + 1) * piece]
                blocks.append((seen.reshape(senders * piece, -1), spread[chunk][j]))
            out.append(mix(blocks, w_out, w_down, n_dp).reshape(senders, piece, cols))
        mixed = moved.astype(jnp.float32) + jnp.concatenate(out, axis=1)
        mixed = mixed.astype(jnp.bfloat16)
        return jnp.concatenate(relative(mixed, me), axis=0)

    return shards


def mix(blocks, w_out, w_down, n_dp):
    rows = blocks[0][0].shape[0]

    def product(first, second):
        seen = jnp.concatenate([blocks[first][0], blocks[second][0]], axis=0)
        units = jnp.concatenate([blocks[first][1], blocks[second][1]], axis=0)
        total = jnp.dot(seen, w_out, preferred_element_type=jnp.float32)
        return total + jnp.dot(units, w_down, preferred_element_type=jnp.float32)

    got = exchange(product(3, 1).astype(jnp.bfloat16), n_dp, 1)
    kept = product(2, 0)
    across = (kept[:rows] + got[:rows].astype(jnp.float32)).astype(jnp.bfloat16)
    across = exchange(across, n_dp, 2)
    return kept[rows:] + got[rows:].astype(jnp.float32) + across.astype(jnp.float32)


def solution(mesh):
    return jax.shard_map(
        make(mesh.shape["dp"], mesh.shape["mp"]),
        mesh=mesh,
        in_specs=(
            P(("group", "dp"), "mp"),
            P("group", None, None),
            P(),
            P("dp", None, "mp"),
            P("dp", "mp"),
            P("dp", "mp"),
            P("dp", "mp"),
        ),
        out_specs=P(("group", "dp"), "mp"),
        check_vma=False,
    )
```

```python
import jax
import jax.numpy as jnp
from jax import lax
from jax.sharding import PartitionSpec as P

HDIM = 128
IMGS = 2
CHUNKS = 2


def layer_norm(values, eps, axes):
    mean = jnp.mean(values, axis=axes, keepdims=True)
    centred = values - mean
    variance = jnp.mean(centred * centred, axis=axes, keepdims=True)
    return centred * lax.rsqrt(variance + eps)


def attend(qkv, same):
    senders, region, _, width = qkv.shape
    heads = width // HDIM
    query_raw, key_raw, values = (
        qkv[:, :, part].reshape(senders, region, heads, HDIM) for part in range(3)
    )
    query_n = layer_norm(query_raw.astype(jnp.float32), 1e-06, -1).astype(jnp.bfloat16)
    key_n = layer_norm(key_raw.astype(jnp.float32), 1e-06, -1).astype(jnp.bfloat16)
    scores = jnp.einsum(
        "sqhd,skhd->shqk", query_n, key_n, preferred_element_type=jnp.float32
    ) * (1.0 / HDIM**0.5)
    probs = jnp.exp(scores) * same[:, None]
    weights = (probs / jnp.sum(probs, axis=-1, keepdims=True)).astype(jnp.bfloat16)
    result = jnp.einsum(
        "shqk,skhd->sqhd", weights, values, preferred_element_type=jnp.float32
    ).astype(jnp.bfloat16)
    return result.reshape(senders, region, width)


def exchange(values, n_dp, step):
    return lax.ppermute(values, "dp", [(index, index ^ step) for index in range(n_dp)])


def relative(values, me):
    count = values.shape[0]
    return [lax.dynamic_index_in_dim(values, me ^ j, 0, keepdims=False) for j in range(count)]


def product_sum(blocks, weights, n_dp):
    far = jnp.concatenate([blocks[3], blocks[1]], axis=0)
    near = jnp.concatenate([blocks[2], blocks[0]], axis=0)
    rows = blocks[0].shape[0]
    sent = jnp.dot(far, weights, preferred_element_type=jnp.float32).astype(jnp.bfloat16)
    got = exchange(sent, n_dp, 1)
    kept = jnp.dot(near, weights, preferred_element_type=jnp.float32)
    across = (kept[:rows] + got[:rows].astype(jnp.float32)).astype(jnp.bfloat16)
    crossed = exchange(across, n_dp, 2)
    total = kept[rows:] + got[rows:].astype(jnp.float32) + crossed.astype(jnp.float32)
    return total, across


def after(values, earlier):
    return lax.optimization_barrier((values, earlier))[0]


def make(n_dp, n_mp):
    assert n_dp == 4 and n_mp % n_dp == 0
    each = n_mp // n_dp

    def gather(values):
        return lax.all_gather(values, "mp", axis=0, tiled=False)

    def spread_out(gathered, me):
        _, rows, cols = gathered.shape
        gathered = gathered.reshape(n_dp, each, rows, cols)
        parts = relative(gathered, me)
        got = [parts[0]] + [exchange(parts[k], n_dp, k) for k in range(1, n_dp)]
        return [part.transpose(1, 0, 2).reshape(rows, each * cols) for part in got]

    def shards(tokens, counts, ln_gain, w_qkv, w_up, w_out, w_down):
        rows, cols = tokens.shape
        depth, _, part_cols = w_qkv.shape
        senders = counts.shape[0]
        region = rows // senders
        piece = region // CHUNKS
        me = lax.axis_index("dp")
        w_qkv = w_qkv.reshape(depth, 3 * part_cols)

        by_receiver = relative(tokens.reshape(senders, region, cols), me)
        own = jnp.stack(by_receiver, axis=0)
        gain = ln_gain.reshape(n_dp, each, 1, 1, cols)

        def cut(chunk):
            return own[:, chunk * piece : (chunk + 1) * piece].reshape(senders * piece, cols)

        def feed(gathered, earlier=None):
            gathered = gathered.reshape(n_dp, each, senders * piece, cols)
            normed = layer_norm(gathered.astype(jnp.float32), 1e-06, (0, 1, 3))
            normed = (normed * gain.reshape(n_dp, each, 1, cols)).astype(jnp.bfloat16)
            if earlier is not None:
                normed = after(normed, earlier)
            parts = relative(normed, me)
            got = [parts[0]] + [exchange(parts[k], n_dp, k) for k in range(1, n_dp)]
            got = [
                part.transpose(1, 0, 2).reshape(senders, piece, each * cols) for part in got
            ]
            return [
                jnp.concatenate([got[j ^ i][i] for i in range(senders)], axis=0)
                for j in range(n_dp)
            ]

        all_tokens = [gather(cut(chunk)) for chunk in range(CHUNKS)]
        fed = [feed(all_tokens[0])]
        total, mark = product_sum(fed[0], w_up, n_dp)
        hidden = [jax.nn.gelu(total, approximate=False).astype(jnp.bfloat16)]
        all_hidden = [gather(hidden[0])]
        for chunk in range(1, CHUNKS):
            fed.append(feed(after(all_tokens[chunk], mark), hidden[0]))
        by_receiver = after(by_receiver, fed[-1])
        moved = [by_receiver[0]] + [exchange(by_receiver[i], n_dp, i) for i in range(1, senders)]
        moved = jnp.stack(moved, axis=0)

        qkv = []
        for chunk in range(CHUNKS):
            total, mark = product_sum(after(fed[chunk], mark), w_qkv, n_dp)
            qkv.append(total.astype(jnp.bfloat16).reshape(senders, piece, 3, part_cols))
        for chunk in range(1, CHUNKS):
            total, mark = product_sum(after(fed[chunk], mark), w_up, n_dp)
            hidden.append(jax.nn.gelu(total, approximate=False).astype(jnp.bfloat16))

        order = jnp.arange(senders) ^ me
        theirs = lax.dynamic_index_in_dim(counts, me, axis=1, keepdims=False)[order]
        bounds = jnp.cumsum(theirs, axis=-1)
        position = jnp.arange(region)
        segment = jnp.sum((position[None, :, None] >= bounds[:, None, :]).astype(jnp.int32), axis=-1)
        same = (segment[:, :, None] == segment[:, None, :]).astype(jnp.float32)

        qkv = jnp.concatenate(qkv, axis=1)
        if part_cols % HDIM:
            everything = lax.all_gather(qkv, "mp", axis=3, tiled=True)
            attended = attend(everything, same)
            attended = lax.dynamic_slice_in_dim(
                attended, lax.axis_index("mp") * part_cols, part_cols, axis=2
            )
        else:
            attended = attend(qkv, same)

        all_attended = gather(attended.reshape(rows, part_cols))
        for chunk in range(1, CHUNKS):
            all_hidden.append(gather(after(hidden[chunk], (attended, moved))))
        first = spread_out(all_hidden[0], me)
        looked = spread_out(after(all_attended, first), me)
        out = []
        for chunk in range(CHUNKS):
            if chunk:
                spread = spread_out(after(all_hidden[chunk], out[-1]), me)
            else:
                spread = first
            blocks = []
            for j in range(n_dp):
                seen = looked[j].reshape(senders, region, -1)
                seen = seen[:, chunk * piece : (chunk + 1) * piece]
                blocks.append((seen.reshape(senders * piece, -1), spread[j]))
            out.append(mix(blocks, w_out, w_down, n_dp).reshape(senders, piece, cols))
        mixed = moved.astype(jnp.float32) + jnp.concatenate(out, axis=1)
        mixed = mixed.astype(jnp.bfloat16)
        return jnp.concatenate(relative(mixed, me), axis=0)

    return shards


def mix(blocks, w_out, w_down, n_dp):
    rows = blocks[0][0].shape[0]

    def product(first, second):
        seen = jnp.concatenate([blocks[first][0], blocks[second][0]], axis=0)
        units = jnp.concatenate([blocks[first][1], blocks[second][1]], axis=0)
        total = jnp.dot(seen, w_out, preferred_element_type=jnp.float32)
        return total + jnp.dot(units, w_down, preferred_element_type=jnp.float32)

    got = exchange(product(3, 1).astype(jnp.bfloat16), n_dp, 1)
    kept = product(2, 0)
    across = (kept[:rows] + got[:rows].astype(jnp.float32)).astype(jnp.bfloat16)
    across = exchange(across, n_dp, 2)
    return kept[rows:] + got[rows:].astype(jnp.float32) + across.astype(jnp.float32)


def solution(mesh):
    return jax.shard_map(
        make(mesh.shape["dp"], mesh.shape["mp"]),
        mesh=mesh,
        in_specs=(
            P(("group", "dp"), "mp"),
            P("group", None, None),
            P(),
            P("dp", None, "mp"),
            P("dp", "mp"),
            P("dp", "mp"),
            P("dp", "mp"),
        ),
        out_specs=P(("group", "dp"), "mp"),
        check_vma=False,
    )
```

```python
import jax
import jax.numpy as jnp
from jax import lax
from jax.sharding import PartitionSpec as P

HDIM = 128
IMGS = 2


def layer_norm(values, eps, axes):
    mean = jnp.mean(values, axis=axes, keepdims=True)
    centred = values - mean
    variance = jnp.mean(centred * centred, axis=axes, keepdims=True)
    return centred * lax.rsqrt(variance + eps)


def attend(qkv, same):
    senders, region, _, width = qkv.shape
    heads = width // HDIM
    query_raw, key_raw, values = (
        qkv[:, :, part].reshape(senders, region, heads, HDIM) for part in range(3)
    )
    query_n = layer_norm(query_raw.astype(jnp.float32), 1e-06, -1).astype(jnp.bfloat16)
    key_n = layer_norm(key_raw.astype(jnp.float32), 1e-06, -1).astype(jnp.bfloat16)
    scores = jnp.einsum(
        "sqhd,skhd->shqk", query_n, key_n, preferred_element_type=jnp.float32
    ) * (1.0 / HDIM**0.5)
    probs = jnp.exp(scores) * same[:, None]
    weights = (probs / jnp.sum(probs, axis=-1, keepdims=True)).astype(jnp.bfloat16)
    result = jnp.einsum(
        "shqk,skhd->sqhd", weights, values, preferred_element_type=jnp.float32
    ).astype(jnp.bfloat16)
    return result.reshape(senders, region, width)


def exchange(values, n_dp, step):
    return lax.ppermute(values, "dp", [(index, index ^ step) for index in range(n_dp)])


def relative(values, me):
    count = values.shape[0]
    return [lax.dynamic_index_in_dim(values, me ^ j, 0, keepdims=False) for j in range(count)]


def product_sum(blocks, weights, n_dp):
    far = jnp.concatenate([blocks[3], blocks[1]], axis=0)
    near = jnp.concatenate([blocks[2], blocks[0]], axis=0)
    rows = blocks[0].shape[0]
    sent = jnp.dot(far, weights, preferred_element_type=jnp.float32).astype(jnp.bfloat16)
    got = exchange(sent, n_dp, 1)
    kept = jnp.dot(near, weights, preferred_element_type=jnp.float32)
    across = (kept[:rows] + got[:rows].astype(jnp.float32)).astype(jnp.bfloat16)
    crossed = exchange(across, n_dp, 2)
    total = kept[rows:] + got[rows:].astype(jnp.float32) + crossed.astype(jnp.float32)
    return total, across


def after(values, earlier):
    return lax.optimization_barrier((values, earlier))[0]


def make(n_dp, n_mp):
    assert n_dp == 4 and n_mp % n_dp == 0
    each = n_mp // n_dp

    def gather(values):
        return lax.all_gather(values, "mp", axis=0, tiled=False)

    def spread_out(gathered, me):
        _, rows, cols = gathered.shape
        gathered = gathered.reshape(n_dp, each, rows, cols)
        parts = relative(gathered, me)
        got = [parts[0]] + [exchange(parts[k], n_dp, k) for k in range(1, n_dp)]
        return [part.transpose(1, 0, 2).reshape(rows, each * cols) for part in got]

    def shards(tokens, counts, ln_gain, w_qkv, w_up, w_out, w_down):
        rows, cols = tokens.shape
        depth, _, part_cols = w_qkv.shape
        senders = counts.shape[0]
        region = rows // senders
        first = region * 3 // 8
        spans = ((0, first), (first, region))
        me = lax.axis_index("dp")
        w_qkv = w_qkv.reshape(depth, 3 * part_cols)

        by_receiver = relative(tokens.reshape(senders, region, cols), me)
        own = jnp.stack(by_receiver, axis=0)
        gain = ln_gain.reshape(n_dp, each, 1, 1, cols)

        def cut(chunk):
            return own[:, spans[chunk][0] : spans[chunk][1]].reshape(-1, cols)

        def feed(gathered, earlier=None):
            gathered = gathered.reshape(n_dp, each, -1, cols)
            normed = layer_norm(gathered.astype(jnp.float32), 1e-06, (0, 1, 3))
            normed = (normed * gain.reshape(n_dp, each, 1, cols)).astype(jnp.bfloat16)
            if earlier is not None:
                normed = after(normed, earlier)
            parts = relative(normed, me)
            got = [parts[0]] + [exchange(parts[k], n_dp, k) for k in range(1, n_dp)]
            got = [
                part.transpose(1, 0, 2).reshape(senders, -1, each * cols) for part in got
            ]
            return [
                jnp.concatenate([got[j ^ i][i] for i in range(senders)], axis=0)
                for j in range(n_dp)
            ]

        all_tokens = [gather(cut(chunk)) for chunk in range(2)]
        fed = [feed(all_tokens[0])]
        total, mark = product_sum(fed[0], w_up, n_dp)
        hidden = [jax.nn.gelu(total, approximate=False).astype(jnp.bfloat16)]
        all_hidden = [gather(hidden[0])]
        fed.append(feed(after(all_tokens[1], mark), hidden[0]))
        by_receiver, fed[1] = lax.optimization_barrier((by_receiver, fed[1]))
        total, mark = product_sum(fed[1], w_up, n_dp)
        hidden.append(jax.nn.gelu(total, approximate=False).astype(jnp.bfloat16))
        all_hidden.append(gather(hidden[1]))

        qkv = []
        for chunk in range(2):
            total, mark = product_sum(after(fed[chunk], mark), w_qkv, n_dp)
            qkv.append(total.astype(jnp.bfloat16).reshape(senders, -1, 3, part_cols))
        moved = [by_receiver[0]] + [exchange(by_receiver[i], n_dp, i) for i in range(1, senders)]
        moved = jnp.stack(moved, axis=0)

        order = jnp.arange(senders) ^ me
        theirs = lax.dynamic_index_in_dim(counts, me, axis=1, keepdims=False)[order]
        bounds = jnp.cumsum(theirs, axis=-1)
        position = jnp.arange(region)
        segment = jnp.sum((position[None, :, None] >= bounds[:, None, :]).astype(jnp.int32), axis=-1)
        same = (segment[:, :, None] == segment[:, None, :]).astype(jnp.float32)

        qkv = jnp.concatenate(qkv, axis=1)
        if part_cols % HDIM:
            everything = lax.all_gather(qkv, "mp", axis=3, tiled=True)
            attended = attend(everything, same)
            attended = lax.dynamic_slice_in_dim(
                attended, lax.axis_index("mp") * part_cols, part_cols, axis=2
            )
        else:
            attended = attend(qkv, same)

        attended, moved = lax.optimization_barrier((attended, moved))
        all_attended = gather(attended.reshape(rows, part_cols))
        base, mark = [], attended
        for chunk in range(2):
            units = spread_out(after(all_hidden[chunk], mark), me)
            base.append(
                [
                    jnp.dot(
                        jnp.concatenate([units[far], units[near]], axis=0),
                        w_down,
                        preferred_element_type=jnp.float32,
                    )
                    for far, near in ((3, 1), (2, 0))
                ]
            )
            mark = base[-1]
        looked = spread_out(after(all_attended, mark), me)
        out = []
        for chunk, (start, stop) in enumerate(spans):
            seen = [
                part.reshape(senders, region, -1)[:, start:stop].reshape(
                    senders * (stop - start), -1
                )
                for part in looked
            ]
            part = mix(seen, base[chunk], w_out, n_dp)
            out.append(part.reshape(senders, stop - start, cols))
        mixed = moved.astype(jnp.float32) + jnp.concatenate(out, axis=1)
        mixed = mixed.astype(jnp.bfloat16)
        return jnp.concatenate(relative(mixed, me), axis=0)

    return shards


def mix(seen, base, w_out, n_dp):
    rows = seen[0].shape[0]

    def product(first, second, total):
        both = jnp.concatenate([seen[first], seen[second]], axis=0)
        return total + jnp.dot(both, w_out, preferred_element_type=jnp.float32)

    got = exchange(product(3, 1, base[0]).astype(jnp.bfloat16), n_dp, 1)
    kept = product(2, 0, base[1])
    across = (kept[:rows] + got[:rows].astype(jnp.float32)).astype(jnp.bfloat16)
    across = exchange(across, n_dp, 2)
    return kept[rows:] + got[rows:].astype(jnp.float32) + across.astype(jnp.float32)


def solution(mesh):
    return jax.shard_map(
        make(mesh.shape["dp"], mesh.shape["mp"]),
        mesh=mesh,
        in_specs=(
            P(("group", "dp"), "mp"),
            P("group", None, None),
            P(),
            P("dp", None, "mp"),
            P("dp", "mp"),
            P("dp", "mp"),
            P("dp", "mp"),
        ),
        out_specs=P(("group", "dp"), "mp"),
        check_vma=False,
    )
```

```python
import jax
import jax.numpy as jnp
from jax import lax
from jax.sharding import PartitionSpec as P

HDIM = 128
IMGS = 2


def layer_norm(values, eps, axes):
    mean = jnp.mean(values, axis=axes, keepdims=True)
    centred = values - mean
    variance = jnp.mean(centred * centred, axis=axes, keepdims=True)
    return centred * lax.rsqrt(variance + eps)


def attend(qkv, same):
    senders, region, _, width = qkv.shape
    heads = width // HDIM
    query_raw, key_raw, values = (
        qkv[:, :, part].reshape(senders, region, heads, HDIM) for part in range(3)
    )
    query_n = layer_norm(query_raw.astype(jnp.float32), 1e-06, -1).astype(jnp.bfloat16)
    key_n = layer_norm(key_raw.astype(jnp.float32), 1e-06, -1).astype(jnp.bfloat16)
    scores = jnp.einsum(
        "sqhd,skhd->shqk", query_n, key_n, preferred_element_type=jnp.float32
    ) * (1.0 / HDIM**0.5)
    probs = jnp.exp(scores) * same[:, None]
    weights = (probs / jnp.sum(probs, axis=-1, keepdims=True)).astype(jnp.bfloat16)
    result = jnp.einsum(
        "shqk,skhd->sqhd", weights, values, preferred_element_type=jnp.float32
    ).astype(jnp.bfloat16)
    return result.reshape(senders, region, width)


def exchange(values, n_dp, step):
    return lax.ppermute(values, "dp", [(index, index ^ step) for index in range(n_dp)])


def relative(values, me):
    count = values.shape[0]
    return [lax.dynamic_index_in_dim(values, me ^ j, 0, keepdims=False) for j in range(count)]


def product_sum(blocks, weights, n_dp):
    far = jnp.concatenate([blocks[3], blocks[1]], axis=0)
    near = jnp.concatenate([blocks[2], blocks[0]], axis=0)
    rows = blocks[0].shape[0]
    sent = jnp.dot(far, weights, preferred_element_type=jnp.float32).astype(jnp.bfloat16)
    got = exchange(sent, n_dp, 1)
    kept = jnp.dot(near, weights, preferred_element_type=jnp.float32)
    across = (kept[:rows] + got[:rows].astype(jnp.float32)).astype(jnp.bfloat16)
    crossed = exchange(across, n_dp, 2)
    total = kept[rows:] + got[rows:].astype(jnp.float32) + crossed.astype(jnp.float32)
    return total, across


def after(values, earlier):
    return lax.optimization_barrier((values, earlier))[0]


def make(n_dp, n_mp):
    assert n_dp == 4 and n_mp % n_dp == 0
    each = n_mp // n_dp

    def gather(values):
        return lax.all_gather(values, "mp", axis=0, tiled=False)

    def spread_out(gathered, me):
        _, rows, cols = gathered.shape
        gathered = gathered.reshape(n_dp, each, rows, cols)
        parts = relative(gathered, me)
        got = [parts[0]] + [exchange(parts[k], n_dp, k) for k in range(1, n_dp)]
        return [part.transpose(1, 0, 2).reshape(rows, each * cols) for part in got]

    def shards(tokens, counts, ln_gain, w_qkv, w_up, w_out, w_down):
        rows, cols = tokens.shape
        depth, _, part_cols = w_qkv.shape
        senders = counts.shape[0]
        region = rows // senders
        first = region * 3 // 8
        spans = ((0, first), (first, region))
        me = lax.axis_index("dp")
        w_qkv = w_qkv.reshape(depth, 3 * part_cols)

        by_receiver = relative(tokens.reshape(senders, region, cols), me)
        own = jnp.stack(by_receiver, axis=0)
        gain = ln_gain.reshape(n_dp, each, 1, 1, cols)

        def cut(chunk):
            return own[:, spans[chunk][0] : spans[chunk][1]].reshape(-1, cols)

        def feed(gathered):
            gathered = gathered.reshape(n_dp, each, -1, cols)
            normed = layer_norm(gathered.astype(jnp.float32), 1e-06, (0, 1, 3))
            normed = (normed * gain.reshape(n_dp, each, 1, cols)).astype(jnp.bfloat16)
            parts = relative(normed, me)
            got = [parts[0]] + [exchange(parts[k], n_dp, k) for k in range(1, n_dp)]
            got = [
                part.transpose(1, 0, 2).reshape(senders, -1, each * cols) for part in got
            ]
            return [
                jnp.concatenate([got[j ^ i][i] for i in range(senders)], axis=0)
                for j in range(n_dp)
            ]

        all_tokens = [gather(cut(chunk)) for chunk in range(2)]
        fed = [feed(all_tokens[0])]
        total, mark = product_sum(fed[0], w_up, n_dp)
        hidden = [jax.nn.gelu(total, approximate=False).astype(jnp.bfloat16)]
        all_tokens[1], hidden[0] = lax.optimization_barrier((all_tokens[1], hidden[0]))
        all_hidden = [gather(hidden[0])]
        fed.append(feed(all_tokens[1]))
        total, mark = product_sum(fed[1], w_up, n_dp)
        hidden.append(jax.nn.gelu(total, approximate=False).astype(jnp.bfloat16))
        all_hidden[0], hidden[1] = lax.optimization_barrier((all_hidden[0], hidden[1]))
        all_hidden.append(gather(hidden[1]))

        qkv = []
        for chunk in range(2):
            total, mark = product_sum(after(fed[chunk], mark), w_qkv, n_dp)
            qkv.append(total.astype(jnp.bfloat16).reshape(senders, -1, 3, part_cols))
        by_receiver, qkv[1] = lax.optimization_barrier((by_receiver, qkv[1]))
        moved = [by_receiver[0]] + [exchange(by_receiver[i], n_dp, i) for i in range(1, senders)]
        moved = jnp.stack(moved, axis=0)

        order = jnp.arange(senders) ^ me
        theirs = lax.dynamic_index_in_dim(counts, me, axis=1, keepdims=False)[order]
        bounds = jnp.cumsum(theirs, axis=-1)
        position = jnp.arange(region)
        segment = jnp.sum((position[None, :, None] >= bounds[:, None, :]).astype(jnp.int32), axis=-1)
        same = (segment[:, :, None] == segment[:, None, :]).astype(jnp.float32)

        qkv = jnp.concatenate(qkv, axis=1)
        if part_cols % HDIM:
            everything = lax.all_gather(qkv, "mp", axis=3, tiled=True)
            attended = attend(everything, same)
            attended = lax.dynamic_slice_in_dim(
                attended, lax.axis_index("mp") * part_cols, part_cols, axis=2
            )
        else:
            attended = attend(qkv, same)

        attended, moved = lax.optimization_barrier((attended, moved))
        all_attended = gather(attended.reshape(rows, part_cols))
        base, mark = [], attended
        for chunk in range(2):
            units = spread_out(after(all_hidden[chunk], mark), me)
            base.append(
                [
                    jnp.dot(
                        jnp.concatenate([units[far], units[near]], axis=0),
                        w_down,
                        preferred_element_type=jnp.float32,
                    )
                    for far, near in ((3, 1), (2, 0))
                ]
            )
            mark = base[-1]
        looked = spread_out(after(all_attended, mark), me)
        out = []
        for chunk, (start, stop) in enumerate(spans):
            seen = [
                part.reshape(senders, region, -1)[:, start:stop].reshape(
                    senders * (stop - start), -1
                )
                for part in looked
            ]
            part = mix(seen, base[chunk], w_out, n_dp)
            out.append(part.reshape(senders, stop - start, cols))
        mixed = moved.astype(jnp.float32) + jnp.concatenate(out, axis=1)
        mixed = mixed.astype(jnp.bfloat16)
        return jnp.concatenate(relative(mixed, me), axis=0)

    return shards


def mix(seen, base, w_out, n_dp):
    rows = seen[0].shape[0]

    def product(first, second, total):
        both = jnp.concatenate([seen[first], seen[second]], axis=0)
        return total + jnp.dot(both, w_out, preferred_element_type=jnp.float32)

    got = exchange(product(3, 1, base[0]).astype(jnp.bfloat16), n_dp, 1)
    kept = product(2, 0, base[1])
    across = (kept[:rows] + got[:rows].astype(jnp.float32)).astype(jnp.bfloat16)
    across = exchange(across, n_dp, 2)
    return kept[rows:] + got[rows:].astype(jnp.float32) + across.astype(jnp.float32)


def solution(mesh):
    return jax.shard_map(
        make(mesh.shape["dp"], mesh.shape["mp"]),
        mesh=mesh,
        in_specs=(
            P(("group", "dp"), "mp"),
            P("group", None, None),
            P(),
            P("dp", None, "mp"),
            P("dp", "mp"),
            P("dp", "mp"),
            P("dp", "mp"),
        ),
        out_specs=P(("group", "dp"), "mp"),
        check_vma=False,
    )
```
